512 devices in a mesh: ctx: 8 (over y_hi, core), exp: 64 (over x, z, y_lo).
Axes of the slice: x: 4, y: 8 (y_hi: 4, y_lo: 2; y = y_hi * 2 + y_lo), z: 8, core: 2. Of those that a mesh axis runs over, the one named last changes fastest.
Arguments:
- queries: bfloat16 [64, 512, 2048], P('exp', None, 'ctx'), may hold values from -6 to 6
- cache_kv: bfloat16 [64, 512, 512], P('exp', 'ctx'), may hold values from -12 to 12
- new_key_values: bfloat16 [64, 512, 512], P('exp', 'ctx'), may hold values from -12 to 12
- hidden: bfloat16 [64, 512, 2048], P('exp', 'ctx'), may hold values from -6 to 6
- out_weight: bfloat16 [2048, 2048], P('ctx'), may hold values from -0.25 to 0.25
- norm_gain: float32 [2048], replicated, may hold values from 0.1 to 1.9
- routes: int32 [64, 512, 8], P('exp', 'ctx'), may hold values from 0 to 63, all different within a row; in each aligned block of 64 rows (0 to 63, 64 to 127, ..., all dimensions but the last counted through in order) at most 10 rows name the same one
- gate_weights: float32 [64, 512, 8], P('exp', 'ctx'), may hold values from 0.05 to 0.3
- gate_up: bfloat16 [64, 2048, 768], P('exp', 'ctx'), may hold values from -0.125 to 0.125
- down_proj: bfloat16 [64, 2048, 384], P('exp', 'ctx'), may hold values from -0.3125 to 0.3125
Outputs:
- layer_out: bfloat16 [64, 512, 2048], P('exp', 'ctx')
The draws below stay inside these ranges and needn't reach their ends.
Inputs may be any that keep to these rules, and one draw needn't show every extreme that they name: `routes`: each row names 8 different experts; of the 64 rows of one device (aligned blocks of rows, sequences and positions taken in order) at most 10 name the same expert.
All inputs are finite; a program needn't handle non-finite values.
Results may differ from the reference program's by a relative error of at most 0.017.
Values may be sent and summed in bfloat16 or wider, within the bound.
No kernel may reach another device: no remote copies, remote signals or barrier semaphores. Data moves between devices by JAX's collectives and lax.ppermute only.
A program may use at most 64 MiB of HBM per device.

```python
import math
import jax
import jax.numpy as jnp
import numpy as np
from jax import lax

D = 2048
QUERY_HEADS = 16
KEY_VALUE_HEADS = 2
HEAD_WIDTH = 128
FF = 384
TOP = 8
TOK_DEV = 64
EXPERTS = 64
SEQUENCE_COUNT = 64
NEW_TOKENS = 512
CACHED_LENGTH = 512
CAP = 10
N_CTX = 8
N_EXP = 64


def draw_queries(key, part):
    key = jax.random.fold_in(key, 11)
    array_dims = (SEQUENCE_COUNT, NEW_TOKENS, QUERY_HEADS, HEAD_WIDTH)
    base_fill = jnp.clip(0.75 * jax.random.normal(key, array_dims, jnp.float32), -6.0, 6.0)
    return base_fill.reshape(SEQUENCE_COUNT, NEW_TOKENS, QUERY_HEADS * HEAD_WIDTH).astype(jnp.bfloat16)


def draw_cache_kv(key, part):
    key = jax.random.fold_in(key, 23)
    array_dims = (SEQUENCE_COUNT, CACHED_LENGTH, 2, KEY_VALUE_HEADS, HEAD_WIDTH)
    base_fill = jnp.clip(2.0 * jax.random.normal(key, array_dims, jnp.float32), -12.0, 12.0)
    return base_fill.reshape(SEQUENCE_COUNT, CACHED_LENGTH, 2 * KEY_VALUE_HEADS * HEAD_WIDTH).astype(jnp.bfloat16)


def levels(stream_key, shape, pieces, low, top_value):
    factor_of, own = 1.0, jax.random.fold_in(stream_key, 6)
    for dim, shards_of in pieces:
        heights = jnp.exp(jax.random.uniform(jax.random.fold_in(own, dim), (shards_of,), jnp.float32, low / len(pieces), top_value / len(pieces)))
        factor_of = factor_of * jnp.repeat(heights, shape[dim] // shards_of).reshape([-1 if axis == dim else 1 for axis in range(len(shape))])
    return factor_of


def shared_out(stream_key, own, number, rows, count, top, most, skew):
    ranking = jax.random.permutation(stream_key, count)
    crowded, common = portions_of(count, rows * top, most, skew, True), portions_of(count, rows * top, most, skew, False)
    places = jnp.arange(count)

    def named(lengths, offset_by):
        used = int((lengths > 0).sum())
        fixed = max(1, used // 4)
        shifted = fixed + (places - fixed + offset_by * (used - fixed)) % max(1, count - fixed)
        return jnp.zeros((count,), jnp.int32).at[ranking[jnp.where(places < fixed, places, shifted)]].set(jnp.asarray(lengths, jnp.int32))

    lengths = jnp.where(number % 4 == 0, named(crowded, number // 4), named(common, number - number // 4 - 1))
    mixed = jax.random.permutation(jax.random.fold_in(own, 3), count)
    source_of, taker = mixed[0:count // 2 * 2:2], mixed[1:count // 2 * 2:2]
    slack = jnp.minimum(lengths[source_of] - 1, most - lengths[taker]) // 2
    slack = jnp.where((source_of == ranking[0]) | (taker == ranking[0]) | (lengths[taker] == 0), 0, jnp.maximum(slack, 0))
    shifted = jax.random.randint(jax.random.fold_in(own, 4), (count // 2,), 0, 1 << 20) % (slack + 1)
    lengths = lengths.at[source_of].add(-shifted).at[taker].add(shifted)
    items = jnp.searchsorted(jnp.cumsum(lengths), jnp.arange(rows * top), side="right").astype(jnp.int32)
    listing = items.reshape(top, rows).T
    listing = listing[jax.random.permutation(jax.random.fold_in(own, 1), rows)]
    offset_by = jax.random.randint(jax.random.fold_in(own, 2), (rows, 1), 0, top)
    return jnp.take_along_axis(listing, (jnp.arange(top)[None, :] + offset_by) % top, axis=1)


def portions_of(number_of, total, most, skew, full):
    loads = [(1 << 20) // math.isqrt(rank ** skew) + 1 for rank in range(1, number_of + 1)]
    largest = most if full else min(most, max(-(-total // number_of), total * loads[0] // sum(loads)))
    least = 1 if total - largest >= number_of - 1 else 0
    counts, spare = [largest] + [least] * (number_of - 1), total - largest - least * (number_of - 1)
    while spare > 0:
        movable = [i for i in range(1, number_of) if counts[i] < largest] or [i for i in range(1, number_of) if counts[i] < most]
        whole, budget = sum([loads[i] for i in movable]), spare
        for i in movable:
            more = min(most - counts[i], max(1, budget * loads[i] // whole), spare)
            counts[i] = counts[i] + more
            spare = spare - more
    return np.array(counts)


def noise(own_key, shape, deviation, most, pieces=(), kind=jnp.bfloat16):
    values = deviation * jax.random.normal(own_key, shape, jnp.float32)
    if pieces:
        values = values * levels(own_key, shape, pieces, -0.22, 0.18)
    return jnp.clip(values, -most, most).astype(kind)


def setup_inputs(seed: int = 0) -> dict:
    keys = jax.random.split(jax.random.key(seed), 11)
    queries = draw_queries(jax.random.fold_in(keys[10], 71), 0)
    cache_kv = draw_cache_kv(jax.random.fold_in(keys[10], 71), 0)
    new_key_values = noise(keys[2], (SEQUENCE_COUNT, NEW_TOKENS, 2 * KEY_VALUE_HEADS * HEAD_WIDTH), 2.0, 12.0, ((0, 64), (1, 8)))
    hidden = noise(keys[3], (SEQUENCE_COUNT, NEW_TOKENS, D), 1.0, 6.0, ((0, 64), (1, 8)))
    out_weight = noise(keys[4], (QUERY_HEADS * HEAD_WIDTH, D), (QUERY_HEADS * HEAD_WIDTH // 4) ** -0.5, 0.25, ((0, 8),))
    norm_gain = jnp.clip(1.0 + 0.18 * jax.random.normal(keys[5], (D,), jnp.float32), 0.1, 1.9)
    routes_keys = jax.random.split(jax.random.fold_in(keys[6], 1), SEQUENCE_COUNT * NEW_TOKENS // TOK_DEV)
    routes_turns = jax.random.permutation(jax.random.fold_in(keys[6], 3), SEQUENCE_COUNT * NEW_TOKENS // TOK_DEV)
    routes = jax.vmap(lambda own, number: shared_out(jax.random.fold_in(keys[6], 2), own, number, TOK_DEV, EXPERTS, TOP, CAP, 2))(routes_keys, routes_turns).reshape((SEQUENCE_COUNT, NEW_TOKENS, TOP))
    gate_weights = jnp.clip(jnp.exp(math.log(0.3) - 1.7917595 * jax.random.uniform(keys[7], (SEQUENCE_COUNT, NEW_TOKENS, TOP), jnp.float32) ** levels(keys[7], (SEQUENCE_COUNT, NEW_TOKENS, TOP), ((0, 64), (1, 8)), -0.2, 0.2)), 0.05, 0.3)
    gate_up = noise(keys[8], (EXPERTS, D, 2 * FF), D ** -0.5, 0.125, ((0, 64), (1, 8)))
    down_proj = noise(keys[9], (EXPERTS, D, FF), FF ** -0.5, 0.3125, ((0, 64), (1, 8)))
    return dict(queries=queries, cache_kv=cache_kv, new_key_values=new_key_values, hidden=hidden, out_weight=out_weight, norm_gain=norm_gain, routes=routes, gate_weights=gate_weights, gate_up=gate_up, down_proj=down_proj)


norm_epsilon = 1e-06

def attend_sequence(inputs):
    query_rows, cache_rows, span_rows = inputs
    query_group_width = QUERY_HEADS // KEY_VALUE_HEADS
    total_length = CACHED_LENGTH + NEW_TOKENS
    key_value_rows = jnp.concatenate([cache_rows, span_rows], axis=0)
    key_head_rows = jnp.repeat(key_value_rows[:, :KEY_VALUE_HEADS * HEAD_WIDTH].reshape(total_length, KEY_VALUE_HEADS, HEAD_WIDTH), query_group_width, axis=1).astype(jnp.float32)
    value_head_rows = jnp.repeat(key_value_rows[:, KEY_VALUE_HEADS * HEAD_WIDTH:].reshape(total_length, KEY_VALUE_HEADS, HEAD_WIDTH), query_group_width, axis=1).astype(jnp.float32)
    query_heads = query_rows.reshape(NEW_TOKENS, QUERY_HEADS, HEAD_WIDTH).astype(jnp.float32)
    scores = jnp.einsum('qhd,khd->hqk', query_heads, key_head_rows) * HEAD_WIDTH ** (-0.5)
    key_pos = jnp.concatenate([jnp.full((CACHED_LENGTH,), -1, jnp.int32), jnp.arange(NEW_TOKENS, dtype=jnp.int32)])
    visible = key_pos[None, None, :] <= jnp.arange(NEW_TOKENS, dtype=jnp.int32)[None, :, None]
    block_max = lax.optimization_barrier(jnp.max(jnp.where(visible, scores, -1e+30), axis=2))
    probs = jnp.where(visible, jnp.exp(scores - block_max[:, :, None]), 0.0)
    denom = lax.optimization_barrier(jnp.sum(probs, axis=2))
    rounded = lax.optimization_barrier(probs.astype(jnp.bfloat16)).astype(jnp.float32)
    weighted = jnp.einsum('hqk,khd->hqd', rounded, value_head_rows)
    heads_out = (weighted / denom[:, :, None]).astype(jnp.bfloat16)
    return heads_out.transpose(1, 0, 2).reshape(NEW_TOKENS, QUERY_HEADS * HEAD_WIDTH)

def reference(queries, cache_kv, new_key_values, hidden, out_weight, norm_gain, routes, gate_weights, gate_up, down_proj):
    heads_out = lax.map(attend_sequence, (queries, cache_kv, new_key_values)).reshape(SEQUENCE_COUNT * NEW_TOKENS, QUERY_HEADS * HEAD_WIDTH)
    per_group = QUERY_HEADS * HEAD_WIDTH // N_CTX
    head_mix = jnp.zeros((SEQUENCE_COUNT * NEW_TOKENS, D), jnp.float32)
    for index in range(N_CTX):
        partial_mix = jnp.dot(heads_out[:, index * per_group:(index + 1) * per_group], out_weight[index * per_group:(index + 1) * per_group], preferred_element_type=jnp.float32)
        head_mix = head_mix + lax.optimization_barrier(partial_mix.astype(jnp.bfloat16)).astype(jnp.float32)
    residual = hidden.reshape(SEQUENCE_COUNT * NEW_TOKENS, D).astype(jnp.float32) + head_mix
    normed = (residual * lax.rsqrt(lax.optimization_barrier(jnp.mean(residual * residual, axis=1, keepdims=True)) + norm_epsilon) * norm_gain).astype(jnp.bfloat16)
    route_flat = routes.reshape(-1).astype(jnp.int32)
    weight_flat = gate_weights.reshape(-1)
    limit = N_CTX * N_EXP * CAP

    def expert_step(expert, combined):
        matches = route_flat == expert
        picks = jnp.nonzero(matches, size=limit, fill_value=0)[0].astype(jnp.int32)
        valid = jnp.arange(limit, dtype=jnp.int32) < jnp.sum(matches.astype(jnp.int32))
        token_index = picks // TOP
        gathered = normed[token_index]
        gate_and_up = jnp.dot(gathered, gate_up[expert], preferred_element_type=jnp.float32)
        activation = (jax.nn.silu(gate_and_up[:, :FF]) * gate_and_up[:, FF:]).astype(jnp.bfloat16)
        expert_out = jnp.dot(activation, down_proj[expert].T, preferred_element_type=jnp.float32).astype(jnp.bfloat16)
        contrib = jnp.where(valid[:, None], expert_out.astype(jnp.float32) * weight_flat[picks][:, None], 0.0)
        return combined.at[token_index].add(contrib)
    combined = lax.fori_loop(0, EXPERTS, expert_step, jnp.zeros((SEQUENCE_COUNT * NEW_TOKENS, D), jnp.float32))
    return (residual + combined).astype(jnp.bfloat16).reshape(SEQUENCE_COUNT, NEW_TOKENS, D)
```

```python
import jax
import jax.numpy as jnp
from jax import lax
from jax.experimental import pallas as pl
from jax.experimental.pallas import tpu as pltpu
from jax.sharding import Mesh
from jax.sharding import PartitionSpec as P

D = 2048
HEAD_WIDTH = 128
FF = 384
TOK = 64
EXPERTS = 64
CAP = 10
KEYS = 1024
PARTS = 4
WIDTH = D // PARTS
BLOCK = PARTS * CAP
ROWS = EXPERTS * BLOCK
LANES = PARTS * TOK
GROUP = 4
NORM_EPSILON = 1e-06
MIB = 1 << 20

CTX = ("yh", "core")
EXP = ("x", "z", "yl")


def whole(count):
    return [pl.BlockSpec(memory_space=pltpu.VMEM)] * count


def f32_dot(a, b):
    return jnp.dot(a, b, preferred_element_type=jnp.float32)


def iota(shape, dim):
    return lax.broadcasted_iota(jnp.int32, shape, dim)


def attend_kernel(core_ref, q_own, q_other, kv, w_own, w_other, out, heads):
    base = core_ref[0] * TOK
    key_index = iota((4 * TOK, KEYS), 1)
    within = key_index & 127
    key_pos = jnp.where(within < TOK, -1, ((key_index >> 7) * TOK) + within - TOK)
    row_pos = (iota((4 * TOK, KEYS), 0) & (TOK - 1)) + base
    keys = kv[:, :HEAD_WIDTH]
    values = kv[:, HEAD_WIDTH:]
    for block in range(4):
        rows = slice(block * TOK, (block + 1) * TOK)
        q = jnp.concatenate(
            [ref[rows, h * HEAD_WIDTH : (h + 1) * HEAD_WIDTH] for ref in (q_own, q_other) for h in range(2)],
            axis=0,
        )
        scores = lax.dot_general(q, keys, (((1,), (1,)), ((), ())), preferred_element_type=jnp.float32)
        scores = scores * (HEAD_WIDTH**-0.5)
        scores = jnp.where(key_pos <= row_pos + block * 2 * TOK, scores, -1e30)
        peak = jnp.max(scores, axis=1, keepdims=True)
        probs = jnp.exp(scores - peak)
        denom = jnp.sum(probs, axis=1, keepdims=True)
        mixed = (f32_dot(probs.astype(jnp.bfloat16), values) / denom).astype(jnp.bfloat16)
        for h in range(4):
            heads[rows, h * HEAD_WIDTH : (h + 1) * HEAD_WIDTH] = mixed[h * TOK : (h + 1) * TOK]
    out[...] = (f32_dot(heads[:, :256], w_own[...]) + f32_dot(heads[:, 256:], w_other[...])).astype(
        jnp.bfloat16
    )


def attend(core, q_own, q_other, kv, w_own, w_other):
    return pl.pallas_call(
        attend_kernel,
        out_shape=jax.ShapeDtypeStruct((4 * TOK, D), jnp.bfloat16),
        in_specs=[pl.BlockSpec(memory_space=pltpu.SMEM)] + whole(5),
        out_specs=whole(1)[0],
        scratch_shapes=[pltpu.VMEM((4 * TOK, 512), jnp.bfloat16)],
        compiler_params=pltpu.CompilerParams(vmem_limit_bytes=32 * MIB),
        cost_estimate=pl.CostEstimate(flops=10**9, bytes_accessed=4 * MIB, transcendentals=MIB),
        name="attend",
    )(core, q_own, q_other, kv, w_own, w_other)


def routing_kernel(routes, weights, select, combine_hi, combine_lo):
    expert = iota((TOK, EXPERTS), 1)
    routed = jnp.zeros((TOK, EXPERTS), jnp.float32)
    weight = jnp.zeros((TOK, EXPERTS), jnp.float32)
    for k in range(8):
        named = routes[:, k : k + 1] == expert
        routed = jnp.where(named, 1.0, routed)
        weight = jnp.where(named, weights[:, k : k + 1], weight)
    before = (iota((TOK, TOK), 1) < iota((TOK, TOK), 0)).astype(jnp.bfloat16)
    place = f32_dot(before, routed.astype(jnp.bfloat16))
    place = jnp.where(routed > 0, place, -1.0)
    identity = (iota((TOK, TOK), 1) == iota((TOK, TOK), 0)).astype(jnp.bfloat16)
    place_t = lax.dot_general(
        place.astype(jnp.bfloat16), identity, (((0,), (0,)), ((), ())), preferred_element_type=jnp.float32
    )

    def offset(part_slot, column):
        part = (part_slot * 205) >> 11
        slot = part_slot - part * CAP
        return jnp.where(part == (column >> 6), -slot, 100).astype(jnp.float32)

    left = iota((ROWS, 128), 0)
    left_expert = (left * 52429) >> 21
    column = iota((ROWS, 128), 1)
    spread = ((column == left_expert) | (column == left - left_expert * BLOCK + EXPERTS)).astype(jnp.bfloat16)
    table = jnp.concatenate(
        [jnp.concatenate([place_t] * PARTS, axis=1), offset(iota((64, LANES), 0), iota((64, LANES), 1))], axis=0
    ).astype(jnp.bfloat16)
    select[...] = (f32_dot(spread, table) == 0).astype(jnp.bfloat16)

    right = iota((128, ROWS), 1)
    right_expert = (right * 52429) >> 21
    row = iota((128, ROWS), 0)
    spread_t = ((row == right_expert) | (row == right - right_expert * BLOCK + EXPERTS)).astype(jnp.bfloat16)
    table_t = jnp.concatenate(
        [jnp.concatenate([place] * PARTS, axis=0), offset(iota((LANES, 64), 1), iota((LANES, 64), 0))], axis=1
    ).astype(jnp.bfloat16)
    chosen = f32_dot(table_t, spread_t) == 0
    high = weight.astype(jnp.bfloat16)
    low = (weight - high.astype(jnp.float32)).astype(jnp.bfloat16)
    for part, ref in ((high, combine_hi), (low, combine_lo)):
        part = part.astype(jnp.float32)
        wide = jnp.concatenate(
            [jnp.concatenate([part] * PARTS, axis=0), jnp.zeros((LANES, 64), jnp.float32)], axis=1
        ).astype(jnp.bfloat16)
        ref[...] = jnp.where(chosen, f32_dot(wide, spread_t), 0.0).astype(jnp.bfloat16)


def routing(routes, weights):
    return pl.pallas_call(
        routing_kernel,
        out_shape=[
            jax.ShapeDtypeStruct((ROWS, LANES), jnp.bfloat16),
            jax.ShapeDtypeStruct((LANES, ROWS), jnp.bfloat16),
            jax.ShapeDtypeStruct((LANES, ROWS), jnp.bfloat16),
        ],
        in_specs=whole(2),
        out_specs=whole(3),
        compiler_params=pltpu.CompilerParams(vmem_limit_bytes=32 * MIB),
        cost_estimate=pl.CostEstimate(flops=10**9, bytes_accessed=4 * MIB, transcendentals=0),
        name="routing",
    )(routes, weights)


def pack_kernel(shares, hidden, gain, select, rows, residual_out):
    residual = hidden[...].astype(jnp.float32)
    for index in range(4):
        residual = residual + shares[index * TOK : (index + 1) * TOK].astype(jnp.float32)
    residual_out[...] = residual
    scale = lax.rsqrt(jnp.mean(residual * residual, axis=1, keepdims=True) + NORM_EPSILON)
    normed = (residual * scale * gain[...]).astype(jnp.bfloat16)
    tall = jnp.concatenate([normed[:, part * WIDTH : (part + 1) * WIDTH] for part in range(PARTS)], axis=0)
    rows[...] = f32_dot(select[...], tall).astype(jnp.bfloat16)


def pack(shares, hidden, gain, select):
    return pl.pallas_call(
        pack_kernel,
        out_shape=[
            jax.ShapeDtypeStruct((ROWS, WIDTH), jnp.bfloat16),
            jax.ShapeDtypeStruct((TOK, D), jnp.float32),
        ],
        in_specs=whole(4),
        out_specs=whole(2),
        compiler_params=pltpu.CompilerParams(vmem_limit_bytes=32 * MIB),
        cost_estimate=pl.CostEstimate(flops=10**9, bytes_accessed=6 * MIB, transcendentals=64),
        name="pack",
    )(shares, hidden, gain, select)


def order_matrix(inverse):
    size = GROUP * BLOCK
    from_dim, to_dim = (1, 0) if not inverse else (0, 1)
    moved = iota((size, size), to_dim)
    part = (moved * 52429) >> 21
    within = moved - part * (GROUP * CAP)
    source = (within * 205) >> 11
    slot = within - source * CAP
    return (iota((size, size), from_dim) == source * BLOCK + part * CAP + slot).astype(jnp.bfloat16)


def experts_kernel(rows, gate_up, down, out, ordered, activation):
    size = GROUP * BLOCK
    part_rows = GROUP * CAP
    forth = order_matrix(False)
    for pair in range(EXPERTS // GROUP // 2):
        first = pair * 2 * size
        a = f32_dot(forth, rows[first : first + size])
        b = f32_dot(forth, rows[first + size : first + 2 * size])
        for part in range(PARTS):
            piece = slice(part * part_rows, (part + 1) * part_rows)
            ordered[
                pair * 2 * part_rows : (pair + 1) * 2 * part_rows, part * WIDTH : (part + 1) * WIDTH
            ] = jnp.concatenate([a[piece], b[piece]], axis=0).astype(jnp.bfloat16)
    both = f32_dot(ordered[...], gate_up[...])
    gate = both[:, :FF]
    activation[...] = (gate / (1.0 + jnp.exp(-gate)) * both[:, FF:]).astype(jnp.bfloat16)
    for part in range(PARTS):
        columns = slice(part * WIDTH, (part + 1) * WIDTH)
        ordered[:, columns] = lax.dot_general(
            activation[...], down[columns], (((1,), (1,)), ((), ())), preferred_element_type=jnp.float32
        ).astype(jnp.bfloat16)
    back = order_matrix(True)
    for pair in range(EXPERTS // GROUP // 2):
        first = pair * 2 * size
        pieces = [
            ordered[pair * 2 * part_rows : (pair + 1) * 2 * part_rows, part * WIDTH : (part + 1) * WIDTH].astype(
                jnp.float32
            )
            for part in range(PARTS)
        ]
        for half in range(2):
            part_slice = slice(half * part_rows, (half + 1) * part_rows)
            stacked = jnp.concatenate([piece[part_slice] for piece in pieces], axis=0).astype(jnp.bfloat16)
            out[first + half * size : first + (half + 1) * size] = f32_dot(back, stacked).astype(jnp.bfloat16)


def experts(rows, gate_up, down):
    return pl.pallas_call(
        experts_kernel,
        out_shape=jax.ShapeDtypeStruct((ROWS, WIDTH), jnp.bfloat16),
        in_specs=whole(3),
        out_specs=whole(1)[0],
        scratch_shapes=[
            pltpu.VMEM((EXPERTS * CAP, D), jnp.bfloat16),
            pltpu.VMEM((EXPERTS * CAP, FF), jnp.bfloat16),
        ],
        compiler_params=pltpu.CompilerParams(vmem_limit_bytes=40 * MIB),
        cost_estimate=pl.CostEstimate(flops=4 * 10**9, bytes_accessed=10 * MIB, transcendentals=MIB // 4),
        name="experts",
    )(rows, gate_up, down)


def combine_kernel(results, residual, combine_hi, combine_lo, out):
    total = f32_dot(combine_hi[...], results[...]) + f32_dot(combine_lo[...], results[...])
    for part in range(PARTS):
        columns = slice(part * WIDTH, (part + 1) * WIDTH)
        out[:, columns] = (residual[:, columns] + total[part * TOK : (part + 1) * TOK]).astype(jnp.bfloat16)


def combine(results, residual, combine_hi, combine_lo):
    return pl.pallas_call(
        combine_kernel,
        out_shape=jax.ShapeDtypeStruct((TOK, D), jnp.bfloat16),
        in_specs=whole(4),
        out_specs=whole(1)[0],
        compiler_params=pltpu.CompilerParams(vmem_limit_bytes=32 * MIB),
        cost_estimate=pl.CostEstimate(flops=2 * 10**9, bytes_accessed=8 * MIB, transcendentals=0),
        name="combine",
    )(results, residual, combine_hi, combine_lo)


def on_device(
    queries,
    cache_kv,
    new_key_values,
    hidden,
    out_weight,
    norm_gain,
    routes,
    gate_weights,
    gate_up,
    down_proj,
):
    core = lax.axis_index("core")
    swap = [(0, 1), (1, 0)]
    kv_rows = jnp.concatenate([cache_kv[0], new_key_values[0]], axis=0)
    by_head = [
        jnp.concatenate([kv_rows[:, g * 128 : (g + 1) * 128], kv_rows[:, (2 + g) * 128 : (3 + g) * 128]], axis=1)
        for g in range(2)
    ]
    kv = lax.all_to_all(jnp.stack([by_head[0]] * 4 + [by_head[1]] * 4), CTX, 0, 0, tiled=True).reshape(KEYS, 256)
    by_side = queries[0].reshape(4, 2, TOK, 256)
    q_own = lax.dynamic_index_in_dim(by_side, core, 1, False).reshape(4 * TOK, 256)
    q_away = lax.dynamic_index_in_dim(by_side, 1 - core, 1, False).reshape(4 * TOK, 256)
    q_other = lax.ppermute(q_away, "core", swap)
    w_other = lax.ppermute(out_weight, "core", swap)
    select, combine_hi, combine_lo = routing(routes[0], gate_weights[0])
    full_gate_up = lax.all_gather(gate_up[0], CTX, axis=0, tiled=True)
    full_down = lax.all_gather(down_proj[0], CTX, axis=0, tiled=True)

    partial = attend(core.reshape(1), q_own, q_other, kv, out_weight, w_other)
    shares = lax.all_to_all(partial.reshape(4, TOK, D), "yh", 0, 0, tiled=True).reshape(4 * TOK, D)
    rows, residual = pack(shares, hidden[0], norm_gain.reshape(1, D), select)
    arrived = lax.all_to_all(rows.reshape(EXPERTS, BLOCK, WIDTH), EXP, 0, 0, tiled=True)
    outputs = experts(arrived.reshape(ROWS, WIDTH), full_gate_up, full_down)
    results = lax.all_to_all(outputs.reshape(EXPERTS, BLOCK, WIDTH), EXP, 0, 0, tiled=True)
    return combine(results.reshape(ROWS, WIDTH), residual, combine_hi, combine_lo)[None]


def solution(mesh):
    parts = Mesh(mesh.devices.reshape(4, 2, 4, 8, 2), ("yh", "core", "x", "z", "yl"))
    rows = P(EXP, CTX, None)
    return jax.shard_map(
        on_device,
        mesh=parts,
        in_specs=(
            P(EXP, None, CTX),
            rows,
            rows,
            rows,
            P(CTX, None),
            P(),
            rows,
            rows,
            rows,
            rows,
        ),
        out_specs=rows,
        check_vma=False,
    )
```

```python
import jax
import jax.numpy as jnp
from jax import lax
from jax.experimental import pallas as pl
from jax.experimental.pallas import tpu as pltpu
from jax.sharding import Mesh
from jax.sharding import PartitionSpec as P

D = 2048
HEAD_WIDTH = 128
FF = 384
TOK = 64
EXPERTS = 64
CAP = 10
KEYS = 1024
PARTS = 4
WIDTH = D // PARTS
BLOCK = PARTS * CAP
ROWS = EXPERTS * BLOCK
LANES = PARTS * TOK
GROUP = 4
NORM_EPSILON = 1e-06
MIB = 1 << 20

CTX = ("yh", "core")
EXP = ("x", "z", "yl")


def whole(count):
    return [pl.BlockSpec(memory_space=pltpu.VMEM)] * count


def f32_dot(a, b):
    return jnp.dot(a, b, preferred_element_type=jnp.float32)


def iota(shape, dim):
    return lax.broadcasted_iota(jnp.int32, shape, dim)


def prepare_kernel(core_ref, cache, new, queries, kv_out, q_own, q_away, held_kv, held_q, arrivals):
    fetches = [
        pltpu.make_async_copy(cache, held_kv.at[0], arrivals.at[0]),
        pltpu.make_async_copy(new, held_kv.at[1], arrivals.at[1]),
        pltpu.make_async_copy(queries, held_q, arrivals.at[2]),
    ]
    for fetch in fetches:
        fetch.start()
    for fetch in fetches[:2]:
        fetch.wait()
    for head in range(2):
        for index in range(2):
            for half in range(2):
                rows = slice(half * TOK, (half + 1) * TOK)
                kv_out[head * 2 + index, rows, :HEAD_WIDTH] = held_kv[
                    half, :, head * HEAD_WIDTH : (head + 1) * HEAD_WIDTH
                ]
                kv_out[head * 2 + index, rows, HEAD_WIDTH:] = held_kv[
                    half, :, (2 + head) * HEAD_WIDTH : (3 + head) * HEAD_WIDTH
                ]
    fetches[2].wait()
    first = core_ref[0] == 0
    for block in range(4):
        rows = slice(block * TOK, (block + 1) * TOK)
        low = held_q[block * 2 * TOK : (block * 2 + 1) * TOK]
        high = held_q[(block * 2 + 1) * TOK : (block + 1) * 2 * TOK]
        q_own[rows] = jnp.where(first, low, high)
        q_away[rows] = jnp.where(first, high, low)


def prepare(core, cache, new, queries):
    side = jax.ShapeDtypeStruct((4 * TOK, 256), jnp.bfloat16)
    return pl.pallas_call(
        prepare_kernel,
        out_shape=[jax.ShapeDtypeStruct((4, 2 * TOK, 256), jnp.bfloat16), side, side],
        in_specs=[pl.BlockSpec(memory_space=pltpu.SMEM)] + [pl.BlockSpec(memory_space=pl.ANY)] * 3,
        out_specs=whole(3),
        scratch_shapes=[
            pltpu.VMEM((2, TOK, 512), jnp.bfloat16),
            pltpu.VMEM((8 * TOK, 256), jnp.bfloat16),
            pltpu.SemaphoreType.DMA((3,)),
        ],
        compiler_params=pltpu.CompilerParams(vmem_limit_bytes=60 * MIB),
        cost_estimate=pl.CostEstimate(flops=0, bytes_accessed=MIB, transcendentals=0),
        name="prepare",
    )(core, cache, new, queries)


def attend_kernel(core_ref, q_own, q_other, kv, w_own, w_other, out, heads):
    base = core_ref[0] * TOK
    key_index = iota((4 * TOK, KEYS), 1)
    within = key_index & 127
    owner = ((key_index >> 7) & 3) * 2 + (key_index >> 9)
    key_pos = jnp.where(within < TOK, -1, owner * TOK + within - TOK)
    row_pos = (iota((4 * TOK, KEYS), 0) & (TOK - 1)) + base
    keys = kv[:, :HEAD_WIDTH]
    values = kv[:, HEAD_WIDTH:]
    for block in range(4):
        rows = slice(block * TOK, (block + 1) * TOK)
        q = jnp.concatenate(
            [ref[rows, h * HEAD_WIDTH : (h + 1) * HEAD_WIDTH] for ref in (q_own, q_other) for h in range(2)],
            axis=0,
        )
        scores = lax.dot_general(q, keys, (((1,), (1,)), ((), ())), preferred_element_type=jnp.float32)
        scores = scores * (HEAD_WIDTH**-0.5)
        scores = jnp.where(key_pos <= row_pos + block * 2 * TOK, scores, -1e30)
        peak = jnp.max(scores, axis=1, keepdims=True)
        probs = jnp.exp(scores - peak)
        denom = jnp.sum(probs, axis=1, keepdims=True)
        mixed = (f32_dot(probs.astype(jnp.bfloat16), values) / denom).astype(jnp.bfloat16)
        for h in range(4):
            heads[rows, h * HEAD_WIDTH : (h + 1) * HEAD_WIDTH] = mixed[h * TOK : (h + 1) * TOK]
    out[...] = (f32_dot(heads[:, :256], w_own[...]) + f32_dot(heads[:, 256:], w_other[...])).astype(
        jnp.bfloat16
    )


def attend(core, q_own, q_other, kv, w_own, w_other):
    return pl.pallas_call(
        attend_kernel,
        out_shape=jax.ShapeDtypeStruct((4 * TOK, D), jnp.bfloat16),
        in_specs=[pl.BlockSpec(memory_space=pltpu.SMEM)] + whole(5),
        out_specs=whole(1)[0],
        scratch_shapes=[pltpu.VMEM((4 * TOK, 512), jnp.bfloat16)],
        compiler_params=pltpu.CompilerParams(vmem_limit_bytes=32 * MIB),
        cost_estimate=pl.CostEstimate(flops=10**9, bytes_accessed=4 * MIB, transcendentals=MIB),
        name="attend",
    )(core, q_own, q_other, kv, w_own, w_other)


def routing_kernel(routes, weights, select, combine_hi, combine_lo):
    expert = iota((TOK, EXPERTS), 1)
    routed = jnp.zeros((TOK, EXPERTS), jnp.float32)
    weight = jnp.zeros((TOK, EXPERTS), jnp.float32)
    for k in range(8):
        named = routes[:, k : k + 1] == expert
        routed = jnp.where(named, 1.0, routed)
        weight = jnp.where(named, weights[:, k : k + 1], weight)
    before = (iota((TOK, TOK), 1) < iota((TOK, TOK), 0)).astype(jnp.bfloat16)
    place = f32_dot(before, routed.astype(jnp.bfloat16))
    place = jnp.where(routed > 0, place, -1.0)
    identity = (iota((TOK, TOK), 1) == iota((TOK, TOK), 0)).astype(jnp.bfloat16)
    place_t = lax.dot_general(
        place.astype(jnp.bfloat16), identity, (((0,), (0,)), ((), ())), preferred_element_type=jnp.float32
    )

    def offset(part_slot, column):
        part = (part_slot * 205) >> 11
        slot = part_slot - part * CAP
        return jnp.where(part == (column >> 6), -slot, 100).astype(jnp.float32)

    left = iota((ROWS, 128), 0)
    left_expert = (left * 52429) >> 21
    column = iota((ROWS, 128), 1)
    spread = ((column == left_expert) | (column == left - left_expert * BLOCK + EXPERTS)).astype(jnp.bfloat16)
    table = jnp.concatenate(
        [jnp.concatenate([place_t] * PARTS, axis=1), offset(iota((64, LANES), 0), iota((64, LANES), 1))], axis=0
    ).astype(jnp.bfloat16)
    select[...] = (f32_dot(spread, table) == 0).astype(jnp.bfloat16)

    right = iota((128, ROWS), 1)
    right_expert = (right * 52429) >> 21
    row = iota((128, ROWS), 0)
    spread_t = ((row == right_expert) | (row == right - right_expert * BLOCK + EXPERTS)).astype(jnp.bfloat16)
    table_t = jnp.concatenate(
        [jnp.concatenate([place] * PARTS, axis=0), offset(iota((LANES, 64), 1), iota((LANES, 64), 0))], axis=1
    ).astype(jnp.bfloat16)
    chosen = f32_dot(table_t, spread_t) == 0
    high = weight.astype(jnp.bfloat16)
    low = (weight - high.astype(jnp.float32)).astype(jnp.bfloat16)
    for part, ref in ((high, combine_hi), (low, combine_lo)):
        part = part.astype(jnp.float32)
        wide = jnp.concatenate(
            [jnp.concatenate([part] * PARTS, axis=0), jnp.zeros((LANES, 64), jnp.float32)], axis=1
        ).astype(jnp.bfloat16)
        ref[...] = jnp.where(chosen, f32_dot(wide, spread_t), 0.0).astype(jnp.bfloat16)


def routing(routes, weights):
    return pl.pallas_call(
        routing_kernel,
        out_shape=[
            jax.ShapeDtypeStruct((ROWS, LANES), jnp.bfloat16),
            jax.ShapeDtypeStruct((LANES, ROWS), jnp.bfloat16),
            jax.ShapeDtypeStruct((LANES, ROWS), jnp.bfloat16),
        ],
        in_specs=whole(2),
        out_specs=whole(3),
        compiler_params=pltpu.CompilerParams(vmem_limit_bytes=32 * MIB),
        cost_estimate=pl.CostEstimate(flops=10**9, bytes_accessed=4 * MIB, transcendentals=0),
        name="routing",
    )(routes, weights)


def pack_kernel(shares, hidden, gain, select, rows, residual_out):
    residual = hidden[...].astype(jnp.float32)
    for index in range(4):
        residual = residual + shares[index * TOK : (index + 1) * TOK].astype(jnp.float32)
    residual_out[...] = residual
    scale = lax.rsqrt(jnp.mean(residual * residual, axis=1, keepdims=True) + NORM_EPSILON)
    normed = (residual * scale * gain[...]).astype(jnp.bfloat16)
    tall = jnp.concatenate([normed[:, part * WIDTH : (part + 1) * WIDTH] for part in range(PARTS)], axis=0)
    rows[...] = f32_dot(select[...], tall).astype(jnp.bfloat16)


def pack(shares, hidden, gain, select):
    return pl.pallas_call(
        pack_kernel,
        out_shape=[
            jax.ShapeDtypeStruct((ROWS, WIDTH), jnp.bfloat16),
            jax.ShapeDtypeStruct((TOK, D), jnp.float32),
        ],
        in_specs=whole(4),
        out_specs=whole(2),
        compiler_params=pltpu.CompilerParams(vmem_limit_bytes=32 * MIB),
        cost_estimate=pl.CostEstimate(flops=10**9, bytes_accessed=6 * MIB, transcendentals=64),
        name="pack",
    )(shares, hidden, gain, select)


def order_matrix(inverse):
    size = GROUP * BLOCK
    from_dim, to_dim = (1, 0) if not inverse else (0, 1)
    moved = iota((size, size), to_dim)
    part = (moved * 52429) >> 21
    within = moved - part * (GROUP * CAP)
    source = (within * 205) >> 11
    slot = within - source * CAP
    return (iota((size, size), from_dim) == source * BLOCK + part * CAP + slot).astype(jnp.bfloat16)


def experts_kernel(rows, gate_up, down, out, ordered, activation):
    size = GROUP * BLOCK
    part_rows = GROUP * CAP
    forth = order_matrix(False)
    for pair in range(EXPERTS // GROUP // 2):
        first = pair * 2 * size
        a = f32_dot(forth, rows[first : first + size])
        b = f32_dot(forth, rows[first + size : first + 2 * size])
        for part in range(PARTS):
            piece = slice(part * part_rows, (part + 1) * part_rows)
            ordered[
                pair * 2 * part_rows : (pair + 1) * 2 * part_rows, part * WIDTH : (part + 1) * WIDTH
            ] = jnp.concatenate([a[piece], b[piece]], axis=0).astype(jnp.bfloat16)
    both = f32_dot(ordered[...], gate_up[...])
    gate = both[:, :FF]
    activation[...] = (gate / (1.0 + jnp.exp(-gate)) * both[:, FF:]).astype(jnp.bfloat16)
    for part in range(PARTS):
        columns = slice(part * WIDTH, (part + 1) * WIDTH)
        ordered[:, columns] = lax.dot_general(
            activation[...], down[columns], (((1,), (1,)), ((), ())), preferred_element_type=jnp.float32
        ).astype(jnp.bfloat16)
    back = order_matrix(True)
    for pair in range(EXPERTS // GROUP // 2):
        first = pair * 2 * size
        pieces = [
            ordered[pair * 2 * part_rows : (pair + 1) * 2 * part_rows, part * WIDTH : (part + 1) * WIDTH].astype(
                jnp.float32
            )
            for part in range(PARTS)
        ]
        for half in range(2):
            part_slice = slice(half * part_rows, (half + 1) * part_rows)
            stacked = jnp.concatenate([piece[part_slice] for piece in pieces], axis=0).astype(jnp.bfloat16)
            out[first + half * size : first + (half + 1) * size] = f32_dot(back, stacked).astype(jnp.bfloat16)


def experts(rows, gate_up, down):
    return pl.pallas_call(
        experts_kernel,
        out_shape=jax.ShapeDtypeStruct((ROWS, WIDTH), jnp.bfloat16),
        in_specs=whole(3),
        out_specs=whole(1)[0],
        scratch_shapes=[
            pltpu.VMEM((EXPERTS * CAP, D), jnp.bfloat16),
            pltpu.VMEM((EXPERTS * CAP, FF), jnp.bfloat16),
        ],
        compiler_params=pltpu.CompilerParams(vmem_limit_bytes=40 * MIB),
        cost_estimate=pl.CostEstimate(flops=4 * 10**9, bytes_accessed=10 * MIB, transcendentals=MIB // 4),
        name="experts",
    )(rows, gate_up, down)


def combine_kernel(results, residual, combine_hi, combine_lo, out):
    total = f32_dot(combine_hi[...], results[...]) + f32_dot(combine_lo[...], results[...])
    for part in range(PARTS):
        columns = slice(part * WIDTH, (part + 1) * WIDTH)
        out[:, columns] = (residual[:, columns] + total[part * TOK : (part + 1) * TOK]).astype(jnp.bfloat16)


def combine(results, residual, combine_hi, combine_lo):
    return pl.pallas_call(
        combine_kernel,
        out_shape=jax.ShapeDtypeStruct((TOK, D), jnp.bfloat16),
        in_specs=whole(4),
        out_specs=whole(1)[0],
        compiler_params=pltpu.CompilerParams(vmem_limit_bytes=32 * MIB),
        cost_estimate=pl.CostEstimate(flops=2 * 10**9, bytes_accessed=8 * MIB, transcendentals=0),
        name="combine",
    )(results, residual, combine_hi, combine_lo)


def on_device(
    queries,
    cache_kv,
    new_key_values,
    hidden,
    out_weight,
    norm_gain,
    routes,
    gate_weights,
    gate_up,
    down_proj,
):
    core = lax.axis_index("core")
    swap = [(0, 1), (1, 0)]
    kv_send, q_own, q_away = prepare(core.reshape(1), cache_kv[0], new_key_values[0], queries[0])
    kv = lax.all_to_all(kv_send, "yh", 0, 0, tiled=True).reshape(KEYS // 2, 256)
    kv = lax.all_gather(kv, "core", axis=0, tiled=True)
    q_other = lax.ppermute(q_away, "core", swap)
    w_other = lax.ppermute(out_weight, "core", swap)
    select, combine_hi, combine_lo = routing(routes[0], gate_weights[0])
    full_gate_up = lax.all_gather(gate_up[0], CTX, axis=0, tiled=True)
    full_down = lax.all_gather(down_proj[0], CTX, axis=0, tiled=True)
    partial = attend(core.reshape(1), q_own, q_other, kv, out_weight, w_other)
    shares = lax.all_to_all(partial.reshape(4, TOK, D), "yh", 0, 0, tiled=True).reshape(4 * TOK, D)
    rows, residual = pack(shares, hidden[0], norm_gain.reshape(1, D), select)
    arrived = lax.all_to_all(rows.reshape(EXPERTS, BLOCK, WIDTH), EXP, 0, 0, tiled=True)
    outputs = experts(arrived.reshape(ROWS, WIDTH), full_gate_up, full_down)
    results = lax.all_to_all(outputs.reshape(EXPERTS, BLOCK, WIDTH), EXP, 0, 0, tiled=True)
    return combine(results.reshape(ROWS, WIDTH), residual, combine_hi, combine_lo)[None]


def solution(mesh):
    parts = Mesh(mesh.devices.reshape(4, 2, 4, 8, 2), ("yh", "core", "x", "z", "yl"))
    rows = P(EXP, CTX, None)
    return jax.shard_map(
        on_device,
        mesh=parts,
        in_specs=(
            P(EXP, None, CTX),
            rows,
            rows,
            rows,
            P(CTX, None),
            P(),
            rows,
            rows,
            rows,
            rows,
        ),
        out_specs=rows,
        check_vma=False,
    )
```

```python
import jax
import jax.numpy as jnp
from jax import lax
from jax.experimental import pallas as pl
from jax.experimental.pallas import tpu as pltpu
from jax.sharding import Mesh
from jax.sharding import PartitionSpec as P

D = 2048
HEAD_WIDTH = 128
FF = 384
TOK = 64
EXPERTS = 64
CAP = 10
KEYS = 1024
PARTS = 4
WIDTH = D // PARTS
BLOCK = PARTS * CAP
ROWS = EXPERTS * BLOCK
LANES = PARTS * TOK
GROUP = 4
NORM_EPSILON = 1e-06
MIB = 1 << 20

CTX = ("yh", "core")
EXP = ("x", "z", "yl")


def whole(count):
    return [pl.BlockSpec(memory_space=pltpu.VMEM)] * count


def f32_dot(a, b):
    return jnp.dot(a, b, preferred_element_type=jnp.float32)


def iota(shape, dim):
    return lax.broadcasted_iota(jnp.int32, shape, dim)


def prepare_kernel(core_ref, cache, new, queries, kv_out, q_own, q_away, held_kv, held_q, arrivals):
    fetches = [
        pltpu.make_async_copy(cache, held_kv.at[0], arrivals.at[0]),
        pltpu.make_async_copy(new, held_kv.at[1], arrivals.at[1]),
        pltpu.make_async_copy(queries, held_q, arrivals.at[2]),
    ]
    for fetch in fetches:
        fetch.start()
    for fetch in fetches[:2]:
        fetch.wait()
    for head in range(2):
        for index in range(2):
            for half in range(2):
                rows = slice(half * TOK, (half + 1) * TOK)
                kv_out[head * 2 + index, rows, :HEAD_WIDTH] = held_kv[
                    half, :, head * HEAD_WIDTH : (head + 1) * HEAD_WIDTH
                ]
                kv_out[head * 2 + index, rows, HEAD_WIDTH:] = held_kv[
                    half, :, (2 + head) * HEAD_WIDTH : (3 + head) * HEAD_WIDTH
                ]
    fetches[2].wait()
    first = core_ref[0] == 0
    for block in range(4):
        rows = slice(block * TOK, (block + 1) * TOK)
        low = held_q[block * 2 * TOK : (block * 2 + 1) * TOK]
        high = held_q[(block * 2 + 1) * TOK : (block + 1) * 2 * TOK]
        q_own[rows] = jnp.where(first, low, high)
        q_away[rows] = jnp.where(first, high, low)


def prepare(core, cache, new, queries):
    side = jax.ShapeDtypeStruct((4 * TOK, 256), jnp.bfloat16)
    return pl.pallas_call(
        prepare_kernel,
        out_shape=[jax.ShapeDtypeStruct((4, 2 * TOK, 256), jnp.bfloat16), side, side],
        in_specs=[pl.BlockSpec(memory_space=pltpu.SMEM)] + [pl.BlockSpec(memory_space=pl.ANY)] * 3,
        out_specs=whole(3),
        scratch_shapes=[
            pltpu.VMEM((2, TOK, 512), jnp.bfloat16),
            pltpu.VMEM((8 * TOK, 256), jnp.bfloat16),
            pltpu.SemaphoreType.DMA((3,)),
        ],
        compiler_params=pltpu.CompilerParams(vmem_limit_bytes=60 * MIB),
        cost_estimate=pl.CostEstimate(flops=0, bytes_accessed=MIB, transcendentals=0),
        name="prepare",
    )(core, cache, new, queries)


def attend_kernel(core_ref, q_own, q_other, kv, heads):
    base = core_ref[0] * TOK
    key_index = iota((4 * TOK, KEYS), 1)
    within = key_index & 127
    owner = ((key_index >> 7) & 3) * 2 + (key_index >> 9)
    key_pos = jnp.where(within < TOK, -1, owner * TOK + within - TOK)
    row_pos = (iota((4 * TOK, KEYS), 0) & (TOK - 1)) + base
    keys = kv[:, :HEAD_WIDTH]
    values = kv[:, HEAD_WIDTH:]
    for block in range(4):
        rows = slice(block * TOK, (block + 1) * TOK)
        q = jnp.concatenate(
            [ref[rows, h * HEAD_WIDTH : (h + 1) * HEAD_WIDTH] for ref in (q_own, q_other) for h in range(2)],
            axis=0,
        )
        scores = lax.dot_general(q, keys, (((1,), (1,)), ((), ())), preferred_element_type=jnp.float32)
        scores = scores * (HEAD_WIDTH**-0.5)
        scores = jnp.where(key_pos <= row_pos + block * 2 * TOK, scores, -1e30)
        peak = jnp.max(scores, axis=1, keepdims=True)
        probs = jnp.exp(scores - peak)
        denom = jnp.sum(probs, axis=1, keepdims=True)
        mixed = (f32_dot(probs.astype(jnp.bfloat16), values) / denom).astype(jnp.bfloat16)
        for h in range(4):
            heads[rows, h * HEAD_WIDTH : (h + 1) * HEAD_WIDTH] = mixed[h * TOK : (h + 1) * TOK]


def attend(core, q_own, q_other, kv):
    return pl.pallas_call(
        attend_kernel,
        out_shape=jax.ShapeDtypeStruct((4 * TOK, 512), jnp.bfloat16),
        in_specs=[pl.BlockSpec(memory_space=pltpu.SMEM)] + whole(3),
        out_specs=whole(1)[0],
        compiler_params=pltpu.CompilerParams(vmem_limit_bytes=32 * MIB),
        cost_estimate=pl.CostEstimate(flops=4 * 10**9, bytes_accessed=8 * MIB, transcendentals=MIB),
        name="attend",
    )(core, q_own, q_other, kv)


def project_kernel(heads, w_own, w_other, out):
    out[...] = (f32_dot(heads[:, :256], w_own[...]) + f32_dot(heads[:, 256:], w_other[...])).astype(
        jnp.bfloat16
    )


def project(heads, w_own, w_other):
    return pl.pallas_call(
        project_kernel,
        out_shape=jax.ShapeDtypeStruct((4 * TOK, D), jnp.bfloat16),
        in_specs=whole(3),
        out_specs=whole(1)[0],
        compiler_params=pltpu.CompilerParams(vmem_limit_bytes=16 * MIB),
        cost_estimate=pl.CostEstimate(flops=10**9, bytes_accessed=4 * MIB, transcendentals=0),
        name="project",
    )(heads, w_own, w_other)


def routing_kernel(routes, weights, select, combine_hi, combine_lo):
    expert = iota((TOK, EXPERTS), 1)
    routed = jnp.zeros((TOK, EXPERTS), jnp.float32)
    weight = jnp.zeros((TOK, EXPERTS), jnp.float32)
    for k in range(8):
        named = routes[:, k : k + 1] == expert
        routed = jnp.where(named, 1.0, routed)
        weight = jnp.where(named, weights[:, k : k + 1], weight)
    before = (iota((TOK, TOK), 1) < iota((TOK, TOK), 0)).astype(jnp.bfloat16)
    place = f32_dot(before, routed.astype(jnp.bfloat16))
    place = jnp.where(routed > 0, place, -1.0)
    identity = (iota((TOK, TOK), 1) == iota((TOK, TOK), 0)).astype(jnp.bfloat16)
    place_t = lax.dot_general(
        place.astype(jnp.bfloat16), identity, (((0,), (0,)), ((), ())), preferred_element_type=jnp.float32
    )

    def offset(part_slot, column):
        part = (part_slot * 205) >> 11
        slot = part_slot - part * CAP
        return jnp.where(part == (column >> 6), -slot, 100).astype(jnp.float32)

    left = iota((ROWS, 128), 0)
    left_expert = (left * 52429) >> 21
    column = iota((ROWS, 128), 1)
    spread = ((column == left_expert) | (column == left - left_expert * BLOCK + EXPERTS)).astype(jnp.bfloat16)
    table = jnp.concatenate(
        [jnp.concatenate([place_t] * PARTS, axis=1), offset(iota((64, LANES), 0), iota((64, LANES), 1))], axis=0
    ).astype(jnp.bfloat16)
    select[...] = (f32_dot(spread, table) == 0).astype(jnp.bfloat16)

    right = iota((128, ROWS), 1)
    right_expert = (right * 52429) >> 21
    row = iota((128, ROWS), 0)
    spread_t = ((row == right_expert) | (row == right - right_expert * BLOCK + EXPERTS)).astype(jnp.bfloat16)
    table_t = jnp.concatenate(
        [jnp.concatenate([place] * PARTS, axis=0), offset(iota((LANES, 64), 1), iota((LANES, 64), 0))], axis=1
    ).astype(jnp.bfloat16)
    chosen = f32_dot(table_t, spread_t) == 0
    high = weight.astype(jnp.bfloat16)
    low = (weight - high.astype(jnp.float32)).astype(jnp.bfloat16)
    for part, ref in ((high, combine_hi), (low, combine_lo)):
        part = part.astype(jnp.float32)
        wide = jnp.concatenate(
            [jnp.concatenate([part] * PARTS, axis=0), jnp.zeros((LANES, 64), jnp.float32)], axis=1
        ).astype(jnp.bfloat16)
        ref[...] = jnp.where(chosen, f32_dot(wide, spread_t), 0.0).astype(jnp.bfloat16)


def routing(routes, weights):
    return pl.pallas_call(
        routing_kernel,
        out_shape=[
            jax.ShapeDtypeStruct((ROWS, LANES), jnp.bfloat16),
            jax.ShapeDtypeStruct((LANES, ROWS), jnp.bfloat16),
            jax.ShapeDtypeStruct((LANES, ROWS), jnp.bfloat16),
        ],
        in_specs=whole(2),
        out_specs=whole(3),
        compiler_params=pltpu.CompilerParams(vmem_limit_bytes=32 * MIB),
        cost_estimate=pl.CostEstimate(flops=10**9, bytes_accessed=4 * MIB, transcendentals=0),
        name="routing",
    )(routes, weights)


def pack_kernel(shares, hidden, gain, select, rows, residual_out):
    residual = hidden[...].astype(jnp.float32)
    for index in range(4):
        residual = residual + shares[index * TOK : (index + 1) * TOK].astype(jnp.float32)
    residual_out[...] = residual
    scale = lax.rsqrt(jnp.mean(residual * residual, axis=1, keepdims=True) + NORM_EPSILON)
    normed = (residual * scale * gain[...]).astype(jnp.bfloat16)
    tall = jnp.concatenate([normed[:, part * WIDTH : (part + 1) * WIDTH] for part in range(PARTS)], axis=0)
    rows[...] = f32_dot(select[...], tall).astype(jnp.bfloat16)


def pack(shares, hidden, gain, select):
    return pl.pallas_call(
        pack_kernel,
        out_shape=[
            jax.ShapeDtypeStruct((ROWS, WIDTH), jnp.bfloat16),
            jax.ShapeDtypeStruct((TOK, D), jnp.float32),
        ],
        in_specs=whole(4),
        out_specs=whole(2),
        compiler_params=pltpu.CompilerParams(vmem_limit_bytes=32 * MIB),
        cost_estimate=pl.CostEstimate(flops=10**9, bytes_accessed=6 * MIB, transcendentals=64),
        name="pack",
    )(shares, hidden, gain, select)


def order_matrix(inverse):
    size = GROUP * BLOCK
    from_dim, to_dim = (1, 0) if not inverse else (0, 1)
    moved = iota((size, size), to_dim)
    part = (moved * 52429) >> 21
    within = moved - part * (GROUP * CAP)
    source = (within * 205) >> 11
    slot = within - source * CAP
    return (iota((size, size), from_dim) == source * BLOCK + part * CAP + slot).astype(jnp.bfloat16)


def experts_kernel(rows, gate_up, down, out, ordered, activation):
    size = GROUP * BLOCK
    part_rows = GROUP * CAP
    forth = order_matrix(False)
    for pair in range(EXPERTS // GROUP // 2):
        first = pair * 2 * size
        a = f32_dot(forth, rows[first : first + size])
        b = f32_dot(forth, rows[first + size : first + 2 * size])
        for part in range(PARTS):
            piece = slice(part * part_rows, (part + 1) * part_rows)
            ordered[
                pair * 2 * part_rows : (pair + 1) * 2 * part_rows, part * WIDTH : (part + 1) * WIDTH
            ] = jnp.concatenate([a[piece], b[piece]], axis=0).astype(jnp.bfloat16)
    both = f32_dot(ordered[...], gate_up[...])
    gate = both[:, :FF]
    activation[...] = (gate / (1.0 + jnp.exp(-gate)) * both[:, FF:]).astype(jnp.bfloat16)
    for part in range(PARTS):
        columns = slice(part * WIDTH, (part + 1) * WIDTH)
        ordered[:, columns] = lax.dot_general(
            activation[...], down[columns], (((1,), (1,)), ((), ())), preferred_element_type=jnp.float32
        ).astype(jnp.bfloat16)
    back = order_matrix(True)
    for pair in range(EXPERTS // GROUP // 2):
        first = pair * 2 * size
        pieces = [
            ordered[pair * 2 * part_rows : (pair + 1) * 2 * part_rows, part * WIDTH : (part + 1) * WIDTH].astype(
                jnp.float32
            )
            for part in range(PARTS)
        ]
        for half in range(2):
            part_slice = slice(half * part_rows, (half + 1) * part_rows)
            stacked = jnp.concatenate([piece[part_slice] for piece in pieces], axis=0).astype(jnp.bfloat16)
            out[first + half * size : first + (half + 1) * size] = f32_dot(back, stacked).astype(jnp.bfloat16)


def experts(rows, gate_up, down):
    return pl.pallas_call(
        experts_kernel,
        out_shape=jax.ShapeDtypeStruct((ROWS, WIDTH), jnp.bfloat16),
        in_specs=whole(3),
        out_specs=whole(1)[0],
        scratch_shapes=[
            pltpu.VMEM((EXPERTS * CAP, D), jnp.bfloat16),
            pltpu.VMEM((EXPERTS * CAP, FF), jnp.bfloat16),
        ],
        compiler_params=pltpu.CompilerParams(vmem_limit_bytes=40 * MIB),
        cost_estimate=pl.CostEstimate(flops=4 * 10**9, bytes_accessed=10 * MIB, transcendentals=MIB // 4),
        name="experts",
    )(rows, gate_up, down)


def combine_kernel(results, residual, combine_hi, combine_lo, out):
    total = f32_dot(combine_hi[...], results[...]) + f32_dot(combine_lo[...], results[...])
    for part in range(PARTS):
        columns = slice(part * WIDTH, (part + 1) * WIDTH)
        out[:, columns] = (residual[:, columns] + total[part * TOK : (part + 1) * TOK]).astype(jnp.bfloat16)


def combine(results, residual, combine_hi, combine_lo):
    return pl.pallas_call(
        combine_kernel,
        out_shape=jax.ShapeDtypeStruct((TOK, D), jnp.bfloat16),
        in_specs=whole(4),
        out_specs=whole(1)[0],
        compiler_params=pltpu.CompilerParams(vmem_limit_bytes=32 * MIB),
        cost_estimate=pl.CostEstimate(flops=2 * 10**9, bytes_accessed=8 * MIB, transcendentals=0),
        name="combine",
    )(results, residual, combine_hi, combine_lo)


def on_device(
    queries,
    cache_kv,
    new_key_values,
    hidden,
    out_weight,
    norm_gain,
    routes,
    gate_weights,
    gate_up,
    down_proj,
):
    core = lax.axis_index("core")
    swap = [(0, 1), (1, 0)]
    kv_send, q_own, q_away = prepare(core.reshape(1), cache_kv[0], new_key_values[0], queries[0])
    kv = lax.all_to_all(kv_send, "yh", 0, 0, tiled=True).reshape(KEYS // 2, 256)
    kv = lax.all_gather(kv, "core", axis=0, tiled=True)
    q_other = lax.ppermute(q_away, "core", swap)
    w_other = lax.ppermute(out_weight, "core", swap)
    select, combine_hi, combine_lo = routing(routes[0], gate_weights[0])
    full_gate_up = lax.all_gather(gate_up[0], CTX, axis=0, tiled=True)
    full_down = lax.all_gather(down_proj[0], CTX, axis=0, tiled=True)
    partial = project(attend(core.reshape(1), q_own, q_other, kv), out_weight, w_other)
    shares = lax.all_to_all(partial.reshape(4, TOK, D), "yh", 0, 0, tiled=True).reshape(4 * TOK, D)
    rows, residual = pack(shares, hidden[0], norm_gain.reshape(1, D), select)
    arrived = lax.all_to_all(rows.reshape(EXPERTS, BLOCK, WIDTH), EXP, 0, 0, tiled=True)
    outputs = experts(arrived.reshape(ROWS, WIDTH), full_gate_up, full_down)
    results = lax.all_to_all(outputs.reshape(EXPERTS, BLOCK, WIDTH), EXP, 0, 0, tiled=True)
    return combine(results.reshape(ROWS, WIDTH), residual, combine_hi, combine_lo)[None]


def solution(mesh):
    parts = Mesh(mesh.devices.reshape(4, 2, 4, 8, 2), ("yh", "core", "x", "z", "yl"))
    rows = P(EXP, CTX, None)
    return jax.shard_map(
        on_device,
        mesh=parts,
        in_specs=(
            P(EXP, None, CTX),
            rows,
            rows,
            rows,
            P(CTX, None),
            P(),
            rows,
            rows,
            rows,
            rows,
        ),
        out_specs=rows,
        check_vma=False,
    )
```

```python
import jax
import jax.numpy as jnp
from jax import lax
from jax.experimental import pallas as pl
from jax.experimental.pallas import tpu as pltpu
from jax.sharding import Mesh
from jax.sharding import PartitionSpec as P

D = 2048
HEAD_WIDTH = 128
FF = 384
TOK = 64
EXPERTS = 64
CAP = 10
KEYS = 1024
PARTS = 4
WIDTH = D // PARTS
BLOCK = PARTS * CAP
ROWS = EXPERTS * BLOCK
LANES = PARTS * TOK
GROUP = 4
NORM_EPSILON = 1e-06
MIB = 1 << 20

CTX = ("yh", "core")
EXP = ("x", "z", "yl")


def whole(count):
    return [pl.BlockSpec(memory_space=pltpu.VMEM)] * count


def f32_dot(a, b):
    return jnp.dot(a, b, preferred_element_type=jnp.float32)


def iota(shape, dim):
    return lax.broadcasted_iota(jnp.int32, shape, dim)


def prepare_kernel(core_ref, cache, new, queries, kv_out, q_own, q_away, held_kv, held_q, arrivals):
    fetches = [
        pltpu.make_async_copy(cache, held_kv.at[0], arrivals.at[0]),
        pltpu.make_async_copy(new, held_kv.at[1], arrivals.at[1]),
        pltpu.make_async_copy(queries, held_q, arrivals.at[2]),
    ]
    for fetch in fetches:
        fetch.start()
    for fetch in fetches[:2]:
        fetch.wait()
    for head in range(2):
        for index in range(2):
            for half in range(2):
                rows = slice(half * TOK, (half + 1) * TOK)
                kv_out[head * 2 + index, rows, :HEAD_WIDTH] = held_kv[
                    half, :, head * HEAD_WIDTH : (head + 1) * HEAD_WIDTH
                ]
                kv_out[head * 2 + index, rows, HEAD_WIDTH:] = held_kv[
                    half, :, (2 + head) * HEAD_WIDTH : (3 + head) * HEAD_WIDTH
                ]
    fetches[2].wait()
    first = core_ref[0] == 0
    for block in range(4):
        rows = slice(block * TOK, (block + 1) * TOK)
        low = held_q[block * 2 * TOK : (block * 2 + 1) * TOK]
        high = held_q[(block * 2 + 1) * TOK : (block + 1) * 2 * TOK]
        q_own[rows] = jnp.where(first, low, high)
        q_away[rows] = jnp.where(first, high, low)


def prepare(core, cache, new, queries):
    side = jax.ShapeDtypeStruct((4 * TOK, 256), jnp.bfloat16)
    return pl.pallas_call(
        prepare_kernel,
        out_shape=[jax.ShapeDtypeStruct((4, 2 * TOK, 256), jnp.bfloat16), side, side],
        in_specs=[pl.BlockSpec(memory_space=pltpu.SMEM)] + [pl.BlockSpec(memory_space=pl.ANY)] * 3,
        out_specs=whole(3),
        scratch_shapes=[
            pltpu.VMEM((2, TOK, 512), jnp.bfloat16),
            pltpu.VMEM((8 * TOK, 256), jnp.bfloat16),
            pltpu.SemaphoreType.DMA((3,)),
        ],
        compiler_params=pltpu.CompilerParams(vmem_limit_bytes=60 * MIB),
        cost_estimate=pl.CostEstimate(flops=0, bytes_accessed=MIB, transcendentals=0),
        name="prepare",
    )(core, cache, new, queries)


def attend_kernel(core_ref, q_own, q_other, kv, heads):
    base = core_ref[0] * TOK
    key_index = iota((4 * TOK, KEYS), 1)
    within = key_index & 127
    owner = ((key_index >> 7) & 3) * 2 + (key_index >> 9)
    key_pos = jnp.where(within < TOK, -1, owner * TOK + within - TOK)
    row_pos = (iota((4 * TOK, KEYS), 0) & (TOK - 1)) + base
    keys = kv[:, :HEAD_WIDTH]
    values = kv[:, HEAD_WIDTH:]
    for block in range(4):
        rows = slice(block * TOK, (block + 1) * TOK)
        q = jnp.concatenate(
            [ref[rows, h * HEAD_WIDTH : (h + 1) * HEAD_WIDTH] for ref in (q_own, q_other) for h in range(2)],
            axis=0,
        )
        scores = lax.dot_general(q, keys, (((1,), (1,)), ((), ())), preferred_element_type=jnp.float32)
        scores = scores * (HEAD_WIDTH**-0.5)
        scores = jnp.where(key_pos <= row_pos + block * 2 * TOK, scores, -1e30)
        peak = jnp.max(scores, axis=1, keepdims=True)
        probs = jnp.exp(scores - peak)
        denom = jnp.sum(probs, axis=1, keepdims=True)
        mixed = (f32_dot(probs.astype(jnp.bfloat16), values) / denom).astype(jnp.bfloat16)
        for h in range(4):
            heads[rows, h * HEAD_WIDTH : (h + 1) * HEAD_WIDTH] = mixed[h * TOK : (h + 1) * TOK]


def attend(core, q_own, q_other, kv):
    return pl.pallas_call(
        attend_kernel,
        out_shape=jax.ShapeDtypeStruct((4 * TOK, 512), jnp.bfloat16),
        in_specs=[pl.BlockSpec(memory_space=pltpu.SMEM)] + whole(3),
        out_specs=whole(1)[0],
        compiler_params=pltpu.CompilerParams(vmem_limit_bytes=32 * MIB),
        cost_estimate=pl.CostEstimate(flops=4 * 10**9, bytes_accessed=8 * MIB, transcendentals=MIB),
        name="attend",
    )(core, q_own, q_other, kv)


def project_kernel(heads, w_own, w_other, out):
    out[...] = (f32_dot(heads[:, :256], w_own[...]) + f32_dot(heads[:, 256:], w_other[...])).astype(
        jnp.bfloat16
    )


def project(heads, w_own, w_other):
    return pl.pallas_call(
        project_kernel,
        out_shape=jax.ShapeDtypeStruct((4 * TOK, D), jnp.bfloat16),
        in_specs=whole(3),
        out_specs=whole(1)[0],
        compiler_params=pltpu.CompilerParams(vmem_limit_bytes=16 * MIB),
        cost_estimate=pl.CostEstimate(flops=10**9, bytes_accessed=4 * MIB, transcendentals=0),
        name="project",
    )(heads, w_own, w_other)


def routing_kernel(routes, weights, select, combine_hi, combine_lo):
    expert = iota((TOK, EXPERTS), 1)
    routed = jnp.zeros((TOK, EXPERTS), jnp.float32)
    weight = jnp.zeros((TOK, EXPERTS), jnp.float32)
    for k in range(8):
        named = routes[:, k : k + 1] == expert
        routed = jnp.where(named, 1.0, routed)
        weight = jnp.where(named, weights[:, k : k + 1], weight)
    before = (iota((TOK, TOK), 1) < iota((TOK, TOK), 0)).astype(jnp.bfloat16)
    place = f32_dot(before, routed.astype(jnp.bfloat16))
    place = jnp.where(routed > 0, place, -1.0)
    identity = (iota((TOK, TOK), 1) == iota((TOK, TOK), 0)).astype(jnp.bfloat16)
    place_t = lax.dot_general(
        place.astype(jnp.bfloat16), identity, (((0,), (0,)), ((), ())), preferred_element_type=jnp.float32
    )

    def offset(part_slot, column):
        part = (part_slot * 205) >> 11
        slot = part_slot - part * CAP
        return jnp.where(part == (column >> 6), -slot, 100).astype(jnp.float32)

    left = iota((ROWS, 128), 0)
    left_expert = (left * 52429) >> 21
    column = iota((ROWS, 128), 1)
    spread = ((column == left_expert) | (column == left - left_expert * BLOCK + EXPERTS)).astype(jnp.bfloat16)
    table = jnp.concatenate(
        [jnp.concatenate([place_t] * PARTS, axis=1), offset(iota((64, LANES), 0), iota((64, LANES), 1))], axis=0
    ).astype(jnp.bfloat16)
    select[...] = (f32_dot(spread, table) == 0).astype(jnp.bfloat16)

    right = iota((128, ROWS), 1)
    right_expert = (right * 52429) >> 21
    row = iota((128, ROWS), 0)
    spread_t = ((row == right_expert) | (row == right - right_expert * BLOCK + EXPERTS)).astype(jnp.bfloat16)
    table_t = jnp.concatenate(
        [jnp.concatenate([place] * PARTS, axis=0), offset(iota((LANES, 64), 1), iota((LANES, 64), 0))], axis=1
    ).astype(jnp.bfloat16)
    chosen = f32_dot(table_t, spread_t) == 0
    high = weight.astype(jnp.bfloat16)
    low = (weight - high.astype(jnp.float32)).astype(jnp.bfloat16)
    for part, ref in ((high, combine_hi), (low, combine_lo)):
        part = part.astype(jnp.float32)
        wide = jnp.concatenate(
            [jnp.concatenate([part] * PARTS, axis=0), jnp.zeros((LANES, 64), jnp.float32)], axis=1
        ).astype(jnp.bfloat16)
        ref[...] = jnp.where(chosen, f32_dot(wide, spread_t), 0.0).astype(jnp.bfloat16)


def routing(routes, weights):
    return pl.pallas_call(
        routing_kernel,
        out_shape=[
            jax.ShapeDtypeStruct((ROWS, LANES), jnp.bfloat16),
            jax.ShapeDtypeStruct((LANES, ROWS), jnp.bfloat16),
            jax.ShapeDtypeStruct((LANES, ROWS), jnp.bfloat16),
        ],
        in_specs=whole(2),
        out_specs=whole(3),
        compiler_params=pltpu.CompilerParams(vmem_limit_bytes=32 * MIB),
        cost_estimate=pl.CostEstimate(flops=10**9, bytes_accessed=4 * MIB, transcendentals=0),
        name="routing",
    )(routes, weights)


def pack_kernel(shares, hidden, gain, select, rows, residual_out):
    residual = hidden[...].astype(jnp.float32)
    for index in range(4):
        residual = residual + shares[index * TOK : (index + 1) * TOK].astype(jnp.float32)
    residual_out[...] = residual
    scale = lax.rsqrt(jnp.mean(residual * residual, axis=1, keepdims=True) + NORM_EPSILON)
    normed = (residual * scale * gain[...]).astype(jnp.bfloat16)
    tall = jnp.concatenate([normed[:, part * WIDTH : (part + 1) * WIDTH] for part in range(PARTS)], axis=0)
    rows[...] = f32_dot(select[...], tall).astype(jnp.bfloat16)


def pack(shares, hidden, gain, select):
    return pl.pallas_call(
        pack_kernel,
        out_shape=[
            jax.ShapeDtypeStruct((ROWS, WIDTH), jnp.bfloat16),
            jax.ShapeDtypeStruct((TOK, D), jnp.float32),
        ],
        in_specs=whole(4),
        out_specs=whole(2),
        compiler_params=pltpu.CompilerParams(vmem_limit_bytes=32 * MIB),
        cost_estimate=pl.CostEstimate(flops=10**9, bytes_accessed=6 * MIB, transcendentals=64),
        name="pack",
    )(shares, hidden, gain, select)


def order_matrix(inverse):
    size = GROUP * BLOCK
    from_dim, to_dim = (1, 0) if not inverse else (0, 1)
    moved = iota((size, size), to_dim)
    part = (moved * 52429) >> 21
    within = moved - part * (GROUP * CAP)
    source = (within * 205) >> 11
    slot = within - source * CAP
    return (iota((size, size), from_dim) == source * BLOCK + part * CAP + slot).astype(jnp.bfloat16)


def experts_kernel(rows, gate_up, down, out, ordered, activation):
    size = GROUP * BLOCK
    part_rows = GROUP * CAP
    forth = order_matrix(False)
    for pair in range(EXPERTS // GROUP // 2):
        first = pair * 2 * size
        a = f32_dot(forth, rows[first : first + size])
        b = f32_dot(forth, rows[first + size : first + 2 * size])
        for part in range(PARTS):
            piece = slice(part * part_rows, (part + 1) * part_rows)
            ordered[
                pair * 2 * part_rows : (pair + 1) * 2 * part_rows, part * WIDTH : (part + 1) * WIDTH
            ] = jnp.concatenate([a[piece], b[piece]], axis=0).astype(jnp.bfloat16)
    both = f32_dot(ordered[...], gate_up[...])
    gate = both[:, :FF]
    activation[...] = (gate / (1.0 + jnp.exp(-gate)) * both[:, FF:]).astype(jnp.bfloat16)
    for part in range(PARTS):
        columns = slice(part * WIDTH, (part + 1) * WIDTH)
        ordered[:, columns] = lax.dot_general(
            activation[...], down[columns], (((1,), (1,)), ((), ())), preferred_element_type=jnp.float32
        ).astype(jnp.bfloat16)
    back = order_matrix(True)
    for pair in range(EXPERTS // GROUP // 2):
        first = pair * 2 * size
        pieces = [
            ordered[pair * 2 * part_rows : (pair + 1) * 2 * part_rows, part * WIDTH : (part + 1) * WIDTH].astype(
                jnp.float32
            )
            for part in range(PARTS)
        ]
        for half in range(2):
            part_slice = slice(half * part_rows, (half + 1) * part_rows)
            stacked = jnp.concatenate([piece[part_slice] for piece in pieces], axis=0).astype(jnp.bfloat16)
            out[first + half * size : first + (half + 1) * size] = f32_dot(back, stacked).astype(jnp.bfloat16)


def experts(rows, gate_up, down):
    return pl.pallas_call(
        experts_kernel,
        out_shape=jax.ShapeDtypeStruct((ROWS, WIDTH), jnp.bfloat16),
        in_specs=whole(3),
        out_specs=whole(1)[0],
        scratch_shapes=[
            pltpu.VMEM((EXPERTS * CAP, D), jnp.bfloat16),
            pltpu.VMEM((EXPERTS * CAP, FF), jnp.bfloat16),
        ],
        compiler_params=pltpu.CompilerParams(vmem_limit_bytes=40 * MIB),
        cost_estimate=pl.CostEstimate(flops=4 * 10**9, bytes_accessed=10 * MIB, transcendentals=MIB // 4),
        name="experts",
    )(rows, gate_up, down)


def stage_kernel(gate_up, down, up_out, down_out, arrivals):
    fetches = [
        pltpu.make_async_copy(gate_up, up_out, arrivals.at[0]),
        pltpu.make_async_copy(down, down_out, arrivals.at[1]),
    ]
    for fetch in fetches:
        fetch.start()
    for fetch in fetches:
        fetch.wait()


def stage(gate_up, down):
    return pl.pallas_call(
        stage_kernel,
        out_shape=[
            jax.ShapeDtypeStruct((D, 2 * FF), jnp.bfloat16),
            jax.ShapeDtypeStruct((D, FF), jnp.bfloat16),
        ],
        in_specs=[pl.BlockSpec(memory_space=pl.ANY)] * 2,
        out_specs=whole(2),
        scratch_shapes=[pltpu.SemaphoreType.DMA((2,))],
        compiler_params=pltpu.CompilerParams(vmem_limit_bytes=46 * MIB),
        cost_estimate=pl.CostEstimate(flops=0, bytes_accessed=9 * MIB, transcendentals=0),
        name="stage",
    )(gate_up, down)


def combine_kernel(results, residual, combine_hi, combine_lo, out):
    total = f32_dot(combine_hi[...], results[...]) + f32_dot(combine_lo[...], results[...])
    for part in range(PARTS):
        columns = slice(part * WIDTH, (part + 1) * WIDTH)
        out[:, columns] = (residual[:, columns] + total[part * TOK : (part + 1) * TOK]).astype(jnp.bfloat16)


def combine(results, residual, combine_hi, combine_lo):
    return pl.pallas_call(
        combine_kernel,
        out_shape=jax.ShapeDtypeStruct((TOK, D), jnp.bfloat16),
        in_specs=whole(4),
        out_specs=whole(1)[0],
        compiler_params=pltpu.CompilerParams(vmem_limit_bytes=32 * MIB),
        cost_estimate=pl.CostEstimate(flops=2 * 10**9, bytes_accessed=8 * MIB, transcendentals=0),
        name="combine",
    )(results, residual, combine_hi, combine_lo)


def on_device(
    queries,
    cache_kv,
    new_key_values,
    hidden,
    out_weight,
    norm_gain,
    routes,
    gate_weights,
    gate_up,
    down_proj,
):
    core = lax.axis_index("core")
    swap = [(0, 1), (1, 0)]
    kv_send, q_own, q_away = prepare(core.reshape(1), cache_kv[0], new_key_values[0], queries[0])
    kv = lax.all_to_all(kv_send, "yh", 0, 0, tiled=True).reshape(KEYS // 2, 256)
    kv = lax.all_gather(kv, "core", axis=0, tiled=True)
    q_other = lax.ppermute(q_away, "core", swap)
    w_other = lax.ppermute(out_weight, "core", swap)
    select, combine_hi, combine_lo = routing(routes[0], gate_weights[0])
    full_gate_up = lax.all_gather(gate_up[0], CTX, axis=0, tiled=True)
    full_down = lax.all_gather(down_proj[0], CTX, axis=0, tiled=True)
    partial = project(attend(core.reshape(1), q_own, q_other, kv), out_weight, w_other)
    shares = lax.all_to_all(partial.reshape(4, TOK, D), "yh", 0, 0, tiled=True).reshape(4 * TOK, D)
    rows, residual = pack(shares, hidden[0], norm_gain.reshape(1, D), select)
    arrived = lax.all_to_all(rows.reshape(EXPERTS, BLOCK, WIDTH), EXP, 0, 0, tiled=True)
    full_gate_up, full_down = stage(full_gate_up, full_down)
    outputs = experts(arrived.reshape(ROWS, WIDTH), full_gate_up, full_down)
    results = lax.all_to_all(outputs.reshape(EXPERTS, BLOCK, WIDTH), EXP, 0, 0, tiled=True)
    return combine(results.reshape(ROWS, WIDTH), residual, combine_hi, combine_lo)[None]


def solution(mesh):
    parts = Mesh(mesh.devices.reshape(4, 2, 4, 8, 2), ("yh", "core", "x", "z", "yl"))
    rows = P(EXP, CTX, None)
    return jax.shard_map(
        on_device,
        mesh=parts,
        in_specs=(
            P(EXP, None, CTX),
            rows,
            rows,
            rows,
            P(CTX, None),
            P(),
            rows,
            rows,
            rows,
            rows,
        ),
        out_specs=rows,
        check_vma=False,
    )
```
